256 devices in a mesh: ctx: 64 (over z, x, core), head: 4 (over y).
Axes of the slice: x: 4, y: 4, z: 8, core: 2. Of those that a mesh axis runs over, the one named last changes fastest.
Arguments:
- queries: bfloat16 [16384, 4096], P('ctx', 'head'), may hold values from -48 to 48
- keys: bfloat16 [16384, 1024], P('ctx', 'head'), may hold values from -48 to 48
- values: bfloat16 [16384, 1024], P('ctx', 'head'), may hold values from -6 to 6
- lengths: int32 [16], replicated, may hold values from 1 to 2048, 16384 in all
- out_weight: bfloat16 [4096, 4096], P('head'), may hold values from -0.09375 to 0.09375
Outputs:
- attended: bfloat16 [16384, 4096], P('ctx', 'head')
- log_sum: float32 [32, 16384], P('head', 'ctx')
- projected: bfloat16 [16384, 4096], P(('ctx', 'head'))
The draws below stay inside these ranges and needn't reach their ends.
All inputs are finite; a program needn't handle non-finite values.
Results may differ from the reference program's by a relative error of at most 0.015.
Values may be sent and summed in bfloat16 or wider, within the bound.
A program may use at most 64 MiB of HBM per device.

```python
import math
import jax
import jax.numpy as jnp
import numpy as np
from jax import lax

D = 4096
HQ = 32
KV = 8
HD = 128
TOK_DEV = 256
TOKENS = 16384
MOST = 2048
DOCS = 16
REACH = 8
N_CTX = 64
N_HEAD = 4


def shared_base(key):
    raw = jax.random.normal(key, (TOKENS, KV * HD), jnp.float32)
    return jnp.clip(raw, -6.0, 6.0)


def draw_keys(key, part):
    raw = shared_base(key)
    return raw.astype(jnp.bfloat16)


def draw_queries(key, part):
    key = jax.random.fold_in(key, 12)
    fresh = jnp.clip(jax.random.normal(key, (TOKENS, HQ * HD), jnp.float32), -6.0, 6.0)
    return fresh.astype(jnp.bfloat16)


def block_scale(rng, extent, shards, least, largest):
    loudness = 1.0
    for position, shards_of in shards:
        heights = jax.random.uniform(jax.random.fold_in(jax.random.fold_in(rng, 6), position), (shards_of,), jnp.float32, least / len(shards), largest / len(shards))
        loudness = loudness * jnp.repeat(jnp.exp(heights), extent[position] // shards_of).reshape((-1,) + (1,) * (len(extent) - 1 - position))
    return loudness


def profile(count, total, most, skew):
    loads = [(1 << 20) // math.isqrt(rank ** skew) + 1 for rank in range(2, count + 1)]
    rest, given = total - most - (count - 1), [1] * (count - 1)
    while rest > 0:
        free = [i for i in range(count - 1) if given[i] < most]
        whole, budget = sum([loads[i] for i in free]), rest
        for i in free:
            more = min(most - given[i], max(1, budget * loads[i] // whole), rest)
            given[i] = given[i] + more
            rest = rest - more
    return np.array([most] + given)


def ragged(key, number_of, total, most, slope):
    if number_of == 2:
        one = jax.random.randint(key, (), max(1, total - most), min(most, total - 1) + 1)
        return jnp.stack([one, total - one])
    sizes = jnp.asarray(profile(number_of, total, most, slope), jnp.int32)
    pairs = (number_of - 1) // 2
    giver, taker = sizes[1:1 + 2 * pairs:2], sizes[2:2 + 2 * pairs:2]
    room = jnp.minimum(giver - 1, most - taker)
    shifted = jax.random.randint(jax.random.fold_in(key, 1), (pairs,), 0, 1 << 20) % (room + 1)
    sizes = sizes.at[1:1 + 2 * pairs:2].set(giver - shifted).at[2:2 + 2 * pairs:2].set(taker + shifted)
    return sizes[jax.random.permutation(jax.random.fold_in(key, 2), number_of)]


def centred(key, extent, deviation, reach, split=(), kind=jnp.bfloat16):
    gain = block_scale(key, extent, split, -0.22, 0.18) if split else 1.0
    array = jax.random.normal(key, extent, jnp.float32) * deviation * gain
    return jnp.minimum(jnp.maximum(array, -reach), reach).astype(kind)


def setup_inputs(seed: int = 0) -> dict:
    key_of = jax.random.split(jax.random.key(seed), 6)
    return {
        "queries": draw_queries(jax.random.fold_in(key_of[5], 71), 0),
        "keys": draw_keys(jax.random.fold_in(key_of[5], 71), 0),
        "values": centred(key_of[2], (TOKENS, KV * HD), 1.0, 6.0, ((0, 64), (1, 4))),
        "lengths": ragged(key_of[3], DOCS, TOKENS, MOST, 2).astype(jnp.int32),
        "out_weight": centred(key_of[4], (HQ * HD, D), (HQ * HD) ** -0.5, 0.09375, ((0, 4),)),
    }


def doc_index(positions, ends):
    return jnp.sum((ends[None, :] <= positions[:, None]).astype(jnp.int32), axis=1)


def reference(queries, keys, values, lengths, out_weight):
    ends = jnp.cumsum(lengths).astype(jnp.int32)
    group = HQ // KV
    span = (REACH + 1) * TOK_DEV
    scale = HD ** -0.5
    front = jnp.zeros((REACH * TOK_DEV, KV * HD), keys.dtype)
    key_pad = jnp.concatenate([front, keys], axis=0)
    val_pad = jnp.concatenate([front, values], axis=0)

    def one_block(block):
        first = (block * TOK_DEV).astype(jnp.int32)
        qrows = lax.dynamic_slice_in_dim(queries, first, TOK_DEV, 0).reshape(TOK_DEV, KV, group, HD)
        krows = lax.dynamic_slice_in_dim(key_pad, first, span, 0).reshape(span, KV, HD)
        vrows = lax.dynamic_slice_in_dim(val_pad, first, span, 0).reshape(span, KV, HD)
        qpos = first + jnp.arange(TOK_DEV, dtype=jnp.int32)
        kpos = first - REACH * TOK_DEV + jnp.arange(span, dtype=jnp.int32)
        qdoc = doc_index(qpos, ends)
        kdoc = doc_index(kpos, ends)
        mask = (kpos[None, :] <= qpos[:, None]) & (kpos[None, :] >= 0) & (kdoc[None, :] == qdoc[:, None])

        def one_head(index):
            qh = qrows[:, index].astype(jnp.float32)
            kh = krows[:, index].astype(jnp.float32)
            vh = vrows[:, index].astype(jnp.float32)
            score = jnp.einsum('qrd,kd->rqk', qh, kh) * scale
            score = jnp.where(mask[None], score, -jnp.inf)
            top = jnp.max(score, axis=-1)
            expo = jnp.exp(score - top[..., None])
            total = jnp.sum(expo, axis=-1)
            rounded = lax.optimization_barrier(expo.astype(jnp.bfloat16))
            mixed = jnp.einsum('rqk,kd->qrd', rounded.astype(jnp.float32), vh)
            mixed = mixed / total.T[..., None]
            return mixed, top + jnp.log(total)

        mixed, lse = lax.map(one_head, jnp.arange(KV, dtype=jnp.int32))
        out = jnp.transpose(mixed, (1, 0, 2, 3)).reshape(TOK_DEV, HQ * HD).astype(jnp.bfloat16)
        return out, lse.reshape(HQ, TOK_DEV)

    outs, lses = lax.map(one_block, jnp.arange(N_CTX, dtype=jnp.int32))
    attended = outs.reshape(TOKENS, HQ * HD)
    log_sum = jnp.transpose(lses, (1, 0, 2)).reshape(HQ, TOKENS)
    width = HQ * HD // N_HEAD
    projected = jnp.zeros((TOKENS, D), jnp.float32)
    for index in range(N_HEAD):
        partial_sum = jnp.dot(attended[:, index * width:(index + 1) * width], out_weight[index * width:(index + 1) * width], preferred_element_type=jnp.float32)
        rounded = lax.optimization_barrier(partial_sum.astype(jnp.bfloat16))
        projected = projected + rounded.astype(jnp.float32)
    return attended, log_sum, projected.astype(jnp.bfloat16)
```

```python
import jax
import jax.numpy as jnp
from jax import lax
from jax.experimental import pallas as pl
from jax.experimental.pallas import tpu as pltpu
from jax.sharding import PartitionSpec as P

HD = 128
T = 256
NX, NC, NY = 4, 2, 4
ROW = NX * NC
KV, GROUP = 2, 4
HQ = KV * GROUP
DOCS = 16
D = 4096
OWNED = T // NY
COLS = 512
PIECES = D // COLS
HALF = PIECES // 2
FAR = -1e30
MESH = pl.DeviceIdType.MESH
F32, BF16 = jnp.float32, jnp.bfloat16
SCALE = HD**-0.5
LOG2E = 1.4426950408889634


def kernel(
    len_ref, q_hbm, k_hbm, v_hbm, w_hbm,
    att_out, lse_out, proj_out,
    q, kv, w, qaug, kaug, score, top, acc, att, lse, part, far, near, comb, proj,
    q_sem, own_sem, w_sem, out_sem,
    z_send, x_send, sib_send, kv_recv, far_send, far_recv, near_send, near_recv,
):
    ctx, me_y = lax.axis_index("ctx"), lax.axis_index("head")
    depth = lax.axis_size("ctx") // ROW
    z, i8 = ctx // ROW, lax.rem(ctx, ROW)
    x, c = i8 // NC, lax.rem(i8, NC)

    def at_x(d):
        return lax.rem(x + d, NX)

    def dev(zz, xx, cc):
        return (zz * ROW + xx * NC + cc, me_y)

    z_up, z_down = lax.rem(z + 1, depth), lax.rem(z + depth - 1, depth)
    right, left, across = (lax.rem(me_y + d, NY) for d in (1, NY - 1, 2))
    sibling = dev(z, x, 1 - c)

    barrier = pltpu.get_barrier_semaphore()
    peers = [dev(z_up, x, c), dev(z_down, x, c), sibling, (ctx, right), (ctx, left)]
    peers += [dev(z, at_x(d), c) for d in (1, 2, 3)]
    for peer in peers:
        pl.semaphore_signal(barrier, inc=1, device_id=peer, device_id_type=MESH)

    own_src = [k_hbm.at[:, pl.ds(g * HD, HD)] for g in range(KV)]
    own_src += [v_hbm.at[:, pl.ds(g * HD, HD)] for g in range(KV)]
    q_copy = pltpu.make_async_copy(q_hbm, q, q_sem)
    own_copies = [pltpu.make_async_copy(own_src[j], kv.at[ROW, j], own_sem.at[j]) for j in range(2 * KV)]

    def column(i):
        return pl.multiple_of(lax.rem(i, 2) * (D // 2) + (i // 2) * COLS, COLS)

    def w_copy(i):
        return pltpu.make_async_copy(w_hbm.at[:, pl.ds(column(i), COLS)], w.at[i], w_sem.at[i])

    q_copy.start()
    for copy in own_copies:
        copy.start()

    pl.semaphore_wait(barrier, len(peers))

    def remote(src, dst, send, recv, device):
        return pltpu.make_async_remote_copy(
            src_ref=src, dst_ref=dst, send_sem=send, recv_sem=recv, device_id=device, device_id_type=MESH
        )

    def z_copy(j):
        return remote(own_src[j], kv.at[i8, j], z_send.at[j], kv_recv.at[i8, j], dev(z_up, x, c))

    def x_copy(src, d, j):
        return remote(src, kv.at[i8, j], x_send.at[d - 1, j], kv_recv.at[i8, j], dev(z, at_x(d), c))

    def sib_copy(src, slot, d, j):
        return remote(src, kv.at[slot, j], sib_send.at[d, j], kv_recv.at[slot, j], sibling)

    def arrived(slot, j):
        remote(kv.at[slot, j], kv.at[slot, j], z_send.at[j], kv_recv.at[slot, j], sibling).wait_recv()

    for j in range(2 * KV):
        z_copy(j).start()
        for d in (1, 3, 2):
            @pl.when(at_x(d) > x)
            def _():
                x_copy(own_src[j], d, j).start()
        @pl.when(c == 0)
        def _():
            sib_copy(own_src[j], i8, 0, j).start()

    def relay(j):
        arrived(i8, j)
        for d in (1, 3, 2):
            @pl.when(at_x(d) < x)
            def _():
                x_copy(kv.at[i8, j], d, j).start()
        @pl.when(c == 1)
        def _():
            sib_copy(kv.at[i8, j], i8, 0, j).start()

    def forward(j):
        for d in (1, 3, 2):
            slot = at_x(d) * NC + c
            arrived(slot, j)
            sib_copy(kv.at[slot, j], slot, d, j).start()

    def from_sibling(j):
        for d in (1, 3, 2):
            arrived(at_x(d) * NC + 1 - c, j)

    def w_start(i, carry):
        w_copy(i).start()
        return carry

    lax.fori_loop(0, PIECES, w_start, 0)

    lane = lax.broadcasted_iota(jnp.int32, (1, HD), 1)
    first = jnp.zeros((1, HD), jnp.int32)
    last = jnp.zeros((1, HD), jnp.int32)
    end = jnp.int32(0)
    for d in range(DOCS):
        first = jnp.where(lane == d, end, first)
        end = end + len_ref[d]
        last = jnp.where(lane == d, end, last)
    token = lax.broadcasted_iota(jnp.int32, (T, HD), 0)

    def inside(block):
        position = block * T + token
        return (position >= first) & (position < last)

    qaug[...] = jnp.where(inside(ctx), 1.0, 0.0).astype(BF16)

    def slot_of(n):
        d = lax.rem(n, 3) + 1
        row = lax.rem(x + d, NX) * NC
        slot = jnp.where(n < 6, row + c, row + 1 - c)
        slot = jnp.where(n == 0, ROW, slot)
        slot = jnp.where(n == 1, i8, slot)
        return jnp.where(n == 2, x * NC + 1 - c, slot)

    def block_of(n):
        slot = slot_of(n)
        block = jnp.where(slot < i8, z * ROW + slot, (z - 1) * ROW + slot)
        return jnp.where(n == 0, ctx, block)

    def build(n, carry):
        kaug[n] = jnp.where(inside(block_of(n)), 0.0, FAR).astype(BF16)
        return carry

    lax.fori_loop(0, ROW + 1, build, 0)

    def scores(n, g, own):
        slot = slot_of(n)
        keys = jnp.concatenate([kv[slot, g], kaug[n]], axis=1)

        def head(r, carry):
            h = g * GROUP + r
            cols = pl.ds(pl.multiple_of(h * HD, HD), HD)
            queries = jnp.concatenate([q[:, cols], qaug[...]], axis=1)
            s = lax.dot_general(queries, keys, (((1,), (1,)), ((), ())), preferred_element_type=F32)
            if own:
                row = lax.broadcasted_iota(jnp.int32, (T, T), 0)
                col = lax.broadcasted_iota(jnp.int32, (T, T), 1)
                s = jnp.where(col <= row, s, FAR)
            score[n, h] = s
            high = jnp.maximum(s[:, :HD], s[:, HD:])
            top[h] = high if own else jnp.maximum(top[h], high)
            return carry

        lax.fori_loop(0, GROUP, head, 0)

    def scores_of(lo, hi, g):
        def body(n, carry):
            scores(n, g, False)
            return carry

        lax.fori_loop(lo, hi, body, 0)

    relay(0)
    q_copy.wait()
    for copy in own_copies:
        copy.wait()
    scores(0, 0, True)
    relay(1)
    scores(0, 1, True)
    for g in range(KV):
        arrived(x * NC + 1 - c, g)
        scores_of(1, 3, g)
    forward(0)
    relay(2)
    scores_of(3, 6, 0)
    forward(1)
    relay(3)
    scores_of(3, 6, 1)
    for g in range(KV):
        from_sibling(g)
        scores_of(6, 9, g)

    def spread(h, carry):
        top[h] = jnp.broadcast_to(jnp.max(top[h], axis=1, keepdims=True), (T, HD))
        return carry

    lax.fori_loop(0, HQ, spread, 0)

    ones = jnp.ones((3 * T, HD), BF16)

    def mix(group, g):
        values = [kv[slot_of(group * 3 + i), KV + g] for i in range(3)]
        values = jnp.concatenate([jnp.concatenate(values, axis=0), ones], axis=1)

        def head(r, carry):
            h = g * GROUP + r
            high = top[h]
            high = jnp.concatenate([high, high], axis=1)
            weight = [
                jnp.exp2((score[group * 3 + i, h] - high) * (SCALE * LOG2E)).astype(BF16) for i in range(3)
            ]
            mixed = jnp.dot(jnp.concatenate(weight, axis=1), values, preferred_element_type=F32)
            acc[h] = mixed if group == 0 else acc[h] + mixed
            return carry

        lax.fori_loop(0, GROUP, head, 0)

    for g in range(KV):
        arrived(x * NC + 1 - c, KV + g)
        mix(0, g)
    for g in range(KV):
        forward(KV + g)
        mix(1, g)
    for g in range(KV):
        from_sibling(KV + g)
        mix(2, g)

    def finish(h, carry):
        total = acc[h, :, HD:]
        cols = pl.ds(pl.multiple_of(h * HD, HD), HD)
        att[:, cols] = (acc[h, :, :HD] / total).astype(BF16)
        return jnp.where(lane == h, top[h] * SCALE + jnp.log(total), carry)

    sums = lax.fori_loop(0, HQ, finish, jnp.zeros((T, HD), F32))
    lse[...] = sums.T[:HQ]
    att_copy = pltpu.make_async_copy(att, att_out, out_sem.at[0])
    lse_copy = pltpu.make_async_copy(lse, lse_out, out_sem.at[1])

    def rows(y):
        return pl.ds(pl.multiple_of(y * OWNED, OWNED), OWNED)

    def far_copy(i):
        side = lax.rem(i, 2)
        target = jnp.where(side == 0, right, left)
        return remote(part.at[rows(across), pl.ds(column(i), COLS)], far.at[i], far_send.at[i], far_recv.at[i], (ctx, target))

    def near_copy(i):
        side = lax.rem(i, 2)
        target = jnp.where(side == 0, left, right)
        return remote(
            part.at[rows(target), pl.ds(column(i), COLS)], near.at[1 - side, i],
            near_send.at[0, i], near_recv.at[1 - side, i], (ctx, target),
        )

    def comb_copy(i):
        side = lax.rem(i, 2)
        target = jnp.where(side == 0, right, left)
        return remote(comb.at[i], near.at[side, i], near_send.at[1, i], near_recv.at[side, i], (ctx, target))

    def project(i, carry):
        w_copy(i).wait()
        part[:, pl.ds(column(i), COLS)] = jnp.dot(att[...], w[i], preferred_element_type=F32).astype(BF16)
        far_copy(i).start()
        return carry

    lax.fori_loop(0, PIECES, project, 0)
    att_copy.start()
    lse_copy.start()

    def send_near(i, carry):
        near_copy(i).start()
        return carry

    lax.fori_loop(0, PIECES, send_near, 0)

    def combine(i, carry):
        target = jnp.where(lax.rem(i, 2) == 0, right, left)
        far_copy(i).wait_recv()
        mine = part[rows(target), pl.ds(column(i), COLS)].astype(F32)
        comb[i] = (mine + far[i].astype(F32)).astype(BF16)
        comb_copy(i).start()
        return carry

    lax.fori_loop(0, PIECES, combine, 0)

    def proj_copy(i):
        return pltpu.make_async_copy(proj.at[i], proj_out.at[:, pl.ds(column(i), COLS)], out_sem.at[2 + i])

    def total(i, carry):
        near_copy(i).wait_recv()
        comb_copy(i).wait_recv()
        mine = part[rows(me_y), pl.ds(column(i), COLS)].astype(F32)
        proj[i] = (mine + near[0, i].astype(F32) + near[1, i].astype(F32)).astype(BF16)
        proj_copy(i).start()
        return carry

    lax.fori_loop(0, PIECES, total, 0)

    for j in range(2 * KV):
        z_copy(j).wait_send()
        for d in (1, 2, 3):
            x_copy(kv.at[i8, j], d, j).wait_send()
            sib_copy(kv.at[i8, j], i8, d, j).wait_send()
        sib_copy(kv.at[i8, j], i8, 0, j).wait_send()

    def drain(i, carry):
        far_copy(i).wait_send()
        near_copy(i).wait_send()
        comb_copy(i).wait_send()
        proj_copy(i).wait()
        return carry

    lax.fori_loop(0, PIECES, drain, 0)
    att_copy.wait()
    lse_copy.wait()


def local(queries, keys, values, lengths, out_weight):
    hbm = pl.BlockSpec(memory_space=pl.ANY)
    dma = pltpu.SemaphoreType.DMA
    return pl.pallas_call(
        kernel,
        out_shape=(
            jax.ShapeDtypeStruct((T, HQ * HD), BF16),
            jax.ShapeDtypeStruct((HQ, T), F32),
            jax.ShapeDtypeStruct((OWNED, D), BF16),
        ),
        in_specs=[pl.BlockSpec(memory_space=pltpu.SMEM)] + [hbm] * 4,
        out_specs=(hbm,) * 3,
        scratch_shapes=[
            pltpu.VMEM((T, HQ * HD), BF16),
            pltpu.VMEM((ROW + 1, 2 * KV, T, HD), BF16),
            pltpu.VMEM((PIECES, HQ * HD, COLS), BF16),
            pltpu.VMEM((T, HD), BF16),
            pltpu.VMEM((ROW + 1, T, HD), BF16),
            pltpu.VMEM((ROW + 1, HQ, T, T), F32),
            pltpu.VMEM((HQ, T, HD), F32),
            pltpu.VMEM((HQ, T, 2 * HD), F32),
            pltpu.VMEM((T, HQ * HD), BF16),
            pltpu.VMEM((HQ, T), F32),
            pltpu.VMEM((T, D), BF16),
            pltpu.VMEM((PIECES, OWNED, COLS), BF16),
            pltpu.VMEM((2, PIECES, OWNED, COLS), BF16),
            pltpu.VMEM((PIECES, OWNED, COLS), BF16),
            pltpu.VMEM((PIECES, OWNED, COLS), BF16),
            dma, dma((2 * KV,)), dma((PIECES,)), dma((2 + PIECES,)),
            dma((2 * KV,)), dma((3, 2 * KV)), dma((4, 2 * KV)), dma((ROW, 2 * KV)),
            dma((PIECES,)), dma((PIECES,)), dma((2, PIECES)), dma((2, PIECES)),
        ],
        compiler_params=pltpu.CompilerParams(
            collective_id=0, has_side_effects=True, vmem_limit_bytes=56 * 2**20
        ),
    )(lengths, queries, keys, values, out_weight)


def solution(mesh):
    placed = (P("ctx", "head"), P("ctx", "head"), P("ctx", "head"), P(), P("head", None))
    return jax.shard_map(
        local,
        mesh=mesh,
        in_specs=placed,
        out_specs=(P("ctx", "head"), P("head", "ctx"), P(("ctx", "head"), None)),
        check_vma=False,
    )
```

```python
import jax
import jax.numpy as jnp
from jax import lax
from jax.experimental import pallas as pl
from jax.experimental.pallas import tpu as pltpu
from jax.sharding import PartitionSpec as P

HD = 128
T = 256
NX, NC, NY = 4, 2, 4
ROW = NX * NC
KV, GROUP = 2, 4
HQ = KV * GROUP
DOCS = 16
D = 4096
OWNED = T // NY
COLS = 512
PIECES = D // COLS
HALF = PIECES // 2
FAR = -1e30
MESH = pl.DeviceIdType.MESH
F32, BF16 = jnp.float32, jnp.bfloat16
SCALE = HD**-0.5
LOG2E = 1.4426950408889634


def kernel(
    len_ref, q_hbm, k_hbm, v_hbm, w_hbm,
    att, lse, proj,
    q, kv, passing, w, qaug, kaug, score, top, acc, part, far, near, comb,
    q_sem, own_sem, w_sem,
    z_send, x_send, sib_send, kv_recv, pass_recv, far_send, far_recv, near_send, near_recv,
):
    ctx, me_y = lax.axis_index("ctx"), lax.axis_index("head")
    depth = lax.axis_size("ctx") // ROW
    z, i8 = ctx // ROW, lax.rem(ctx, ROW)
    x, c = i8 // NC, lax.rem(i8, NC)

    def head_columns(h):
        return pl.ds(pl.multiple_of(h * HD, HD), HD)

    def at_x(d):
        return lax.rem(x + d, NX)

    def dev(zz, xx, cc):
        return (zz * ROW + xx * NC + cc, me_y)

    z_up, z_down = lax.rem(z + 1, depth), lax.rem(z + depth - 1, depth)
    right, left, across = (lax.rem(me_y + d, NY) for d in (1, NY - 1, 2))
    sibling = dev(z, x, 1 - c)

    barrier = pltpu.get_barrier_semaphore()
    peers = [dev(z_up, x, c), dev(z_down, x, c), sibling, (ctx, right), (ctx, left)]
    x_up, x_down = dev(z, at_x(1), c), dev(z, at_x(NX - 1), c)
    peers += [x_up, x_down]
    for peer in peers:
        pl.semaphore_signal(barrier, inc=1, device_id=peer, device_id_type=MESH)

    own_src = [k_hbm.at[:, pl.ds(g * HD, HD)] for g in range(KV)]
    own_src += [v_hbm.at[:, pl.ds(g * HD, HD)] for g in range(KV)]
    q_copy = pltpu.make_async_copy(q_hbm, q, q_sem)
    own_copies = [pltpu.make_async_copy(own_src[j], kv.at[ROW, j], own_sem.at[j]) for j in range(2 * KV)]

    def column(i):
        return pl.multiple_of(lax.rem(i, 2) * (D // 2) + (i // 2) * COLS, COLS)

    def w_copy(i):
        return pltpu.make_async_copy(w_hbm.at[:, pl.ds(column(i), COLS)], w.at[i], w_sem.at[i])

    q_copy.start()
    for copy in own_copies:
        copy.start()

    pl.semaphore_wait(barrier, len(peers))

    def remote(src, dst, send, recv, device):
        return pltpu.make_async_remote_copy(
            src_ref=src, dst_ref=dst, send_sem=send, recv_sem=recv, device_id=device, device_id_type=MESH
        )

    slots = [origin * NC + c for origin in range(NX)]

    def sib_copy(src, origin, j):
        slot = origin * NC + c
        return remote(src, kv.at[slot, j], sib_send.at[origin, j], kv_recv.at[slot, j], sibling)

    def arrived(slot, j):
        remote(kv.at[slot, j], kv.at[slot, j], z_send.at[0, j], kv_recv.at[slot, j], sibling).wait_recv()

    started = [[] for _ in range(NX)]
    OWN, PREV, RELAY = range(3)
    UP, DOWN = range(2)

    def send(role, copy, *sem):
        copy.start()
        started[role].append(sem)

    def along_x(role, way, kind, src, dst, recv, j):
        target = x_up if way == UP else x_down
        send(role, remote(src, dst, x_send.at[way, kind, j], recv, target), x_send, way, kind, j)

    def block_along_x(role, way, kind, origin, src, j):
        slot = slots[origin]
        along_x(role, way, kind, src, kv.at[slot, j], kv_recv.at[slot, j], j)

    def to_sibling(role, origin, src, j):
        send(role, sib_copy(src, origin, j), sib_send, origin, j)

    def up_z(role, kind, origin, src, j):
        slot = slots[origin]
        send(role, remote(src, kv.at[slot, j], z_send.at[kind, j], kv_recv.at[slot, j], dev(z_up, x, c)), z_send, kind, j)

    def got(role, origin, j, *ways):
        src = kv.at[slots[origin], j]
        arrived(slots[origin], j)
        for way in ways:
            block_along_x(role, way, RELAY, origin, src, j)
        to_sibling(role, origin, src, j)

    def got_prev(role, j, *ways):
        src = kv.at[slots[role], j]
        arrived(slots[role], j)
        for way in ways:
            block_along_x(role, way, PREV, role, src, j)

        @pl.when(c == 1)
        def _():
            sib_copy(src, role, j).start()

    def pass_on(role, which, origin, j):
        remote(passing.at[which, j // 2], passing.at[which, j // 2], z_send.at[0, j], pass_recv.at[which, j // 2], sibling).wait_recv()
        if which == 0:
            block_along_x(role, DOWN, RELAY, origin, passing.at[which, j // 2], j)
        else:
            up_z(role, 1, origin, passing.at[which, j // 2], j)

    def to_pass(role, way, kind, which, src, j):
        along_x(role, way, kind, src, passing.at[which, j // 2], pass_recv.at[which, j // 2], j)

    def own_sends(role, b):
        for j in (b, b + 1):
            src = own_src[j]
            up_z(role, 0, role, src, j)
            if role == 1 and j == b:
                to_pass(role, DOWN, OWN, 0, src, j)
            if role < 3:
                block_along_x(role, UP, OWN, role, src, j)
            if role == 0:
                block_along_x(role, DOWN, OWN, role, src, j)

            @pl.when(c == 0)
            def _():
                sib_copy(src, role, j).start()

    def stage_1(role, b):
        if role == 0:
            pass_on(0, 0, 1, b)
            got_prev(0, b)
        elif role == 1:
            got(1, 0, b, UP)
            got_prev(1, b, DOWN)
        elif role == 2:
            got_prev(2, b, DOWN)
            got(2, 1, b)
        else:
            arrived(slots[2], b)
            to_pass(3, UP, RELAY, 1, kv.at[slots[2], b], b)
            to_sibling(3, 2, kv.at[slots[2], b], b)
            got_prev(3, b, UP, DOWN)
            got(3, 0, b)

    def stage_2(role, b):
        if role == 0:
            pass_on(0, 1, 2, b)
            got_prev(0, b + 1)
        elif role == 1:
            got_prev(1, b + 1, DOWN)
            got(1, 0, b + 1)
        elif role == 2:
            got_prev(2, b + 1, DOWN)
            got(2, 1, b + 1, UP)
        else:
            got_prev(3, b + 1, UP, DOWN)
            got(3, 0, b + 1, DOWN)
            got(3, 2, b + 1)

    def stage_3(role, b):
        if role == 0:
            got(0, 3, b, UP)
            got(0, 1, b)
            got(0, 1, b + 1)
            got(0, 2, b)
        elif role == 1:
            got(1, 2, b)
            got(1, 2, b + 1, DOWN)
        elif role == 2:
            got(2, 3, b)
            got(2, 3, b + 1, DOWN)
            got(2, 0, b)
        else:
            got(3, 1, b)
            got(3, 1, b + 1)

    def stage_4(role, b):
        if role == 0:
            got(0, 3, b + 1)
            got(0, 2, b + 1)
        elif role == 1:
            got(1, 3, b)
            got(1, 3, b + 1)
        elif role == 2:
            got(2, 0, b + 1)

    def in_role(stage, b):
        for role in range(NX):
            @pl.when(x == role)
            def _():
                stage(role, b)

    in_role(own_sends, 0)

    def from_sibling(j):
        for d in (1, 3, 2):
            arrived(at_x(d) * NC + 1 - c, j)

    def w_start(i, carry):
        w_copy(i).start()
        return carry

    lax.fori_loop(0, PIECES, w_start, 0)

    lane = lax.broadcasted_iota(jnp.int32, (1, HD), 1)
    first = jnp.zeros((1, HD), jnp.int32)
    last = jnp.zeros((1, HD), jnp.int32)
    end = jnp.int32(0)
    for d in range(DOCS):
        first = jnp.where(lane == d, end, first)
        end = end + len_ref[d]
        last = jnp.where(lane == d, end, last)
    token = lax.broadcasted_iota(jnp.int32, (T, HD), 0)

    def inside(block):
        position = block * T + token
        return (position >= first) & (position < last)

    qaug[...] = jnp.where(inside(ctx), 1.0, 0.0).astype(BF16)

    same_slots = [at_x(d) * NC + c for d in (1, 2, 3)]
    other_slots = [at_x(d) * NC + 1 - c for d in (1, 2, 3)]
    block_slots = [ROW + 0 * x, i8, x * NC + 1 - c] + same_slots + other_slots

    def slot_of(n):
        return block_slots[n]

    for n in range(ROW + 1):
        slot = slot_of(n)
        block = jnp.where(slot < i8, z * ROW + slot, (z - 1) * ROW + slot)
        kaug[n] = jnp.where(inside(ctx if n == 0 else block), 0.0, FAR).astype(BF16)

    def scores(first_n, last_n, g):
        for n in range(first_n, last_n):
            keys = jnp.concatenate([kv[slot_of(n), g], kaug[n]], axis=1)
            for r in range(GROUP):
                h = g * GROUP + r
                queries = jnp.concatenate([q[:, head_columns(h)], qaug[...]], axis=1)
                s = lax.dot_general(queries, keys, (((1,), (1,)), ((), ())), preferred_element_type=F32)
                if n == 0:
                    row = lax.broadcasted_iota(jnp.int32, (T, T), 0)
                    col = lax.broadcasted_iota(jnp.int32, (T, T), 1)
                    s = jnp.where(col <= row, s, FAR)
                score[n, h] = s
                high = jnp.maximum(s[:, :HD], s[:, HD:])
                top[h] = high if n == 0 else jnp.maximum(top[h], high)

    def mix(first_n, g):
        values = [kv[slot_of(first_n + i), KV + g] for i in range(3)]
        values = jnp.concatenate([jnp.concatenate(values, axis=0), jnp.ones((3 * T, HD), BF16)], axis=1)
        for r in range(GROUP):
            h = g * GROUP + r
            high = jnp.concatenate([top[h], top[h]], axis=1)
            weight = [jnp.exp2((score[first_n + i, h] - high) * (SCALE * LOG2E)).astype(BF16) for i in range(3)]
            mixed = jnp.dot(jnp.concatenate(weight, axis=1), values, preferred_element_type=F32)
            acc[h] = mixed if first_n == 0 else acc[h] + mixed

    q_copy.wait()
    for copy in own_copies:
        copy.wait()

    def own_scores(g, carry):
        scores(0, 1, g)
        return carry

    def close_scores(g, carry):
        arrived(x * NC + 1 - c, g)
        scores(1, 3, g)
        return carry

    def same_scores(g, carry):
        scores(3, 6, g)
        return carry

    def other_scores(g, carry):
        from_sibling(g)
        scores(6, 9, g)
        return carry

    def close_mix(g, carry):
        arrived(x * NC + 1 - c, KV + g)
        mix(0, g)
        return carry

    def same_mix(g, carry):
        mix(3, g)
        return carry

    def other_mix(g, carry):
        from_sibling(KV + g)
        mix(6, g)
        return carry

    def each_kv(step):
        lax.fori_loop(0, KV, step, 0)

    each_kv(own_scores)
    in_role(stage_1, 0)
    in_role(own_sends, KV)
    in_role(stage_2, 0)
    each_kv(close_scores)
    in_role(stage_3, 0)
    in_role(stage_1, KV)
    in_role(stage_4, 0)
    in_role(stage_2, KV)
    each_kv(same_scores)
    each_kv(other_scores)
    for h in range(HQ):
        top[h] = jnp.broadcast_to(jnp.max(top[h], axis=1, keepdims=True), (T, HD))
    in_role(stage_3, KV)
    each_kv(close_mix)
    in_role(stage_4, KV)
    each_kv(same_mix)
    each_kv(other_mix)

    sums = jnp.zeros((T, HD), F32)
    for h in range(HQ):
        total = acc[h, :, HD:]
        att[:, h * HD : (h + 1) * HD] = (acc[h, :, :HD] / total).astype(BF16)
        sums = jnp.where(lane == h, top[h] * SCALE + jnp.log(total), sums)
    lse[...] = sums.T[:HQ]

    def rows(y):
        return pl.ds(pl.multiple_of(y * OWNED, OWNED), OWNED)

    def far_copy(i):
        side = lax.rem(i, 2)
        target = jnp.where(side == 0, right, left)
        return remote(part.at[rows(across), pl.ds(column(i), COLS)], far.at[i], far_send.at[i], far_recv.at[i], (ctx, target))

    def near_copy(i):
        side = lax.rem(i, 2)
        target = jnp.where(side == 0, left, right)
        return remote(
            part.at[rows(target), pl.ds(column(i), COLS)], near.at[1 - side, i],
            near_send.at[0, i], near_recv.at[1 - side, i], (ctx, target),
        )

    def comb_copy(i):
        side = lax.rem(i, 2)
        target = jnp.where(side == 0, right, left)
        return remote(comb.at[i], near.at[side, i], near_send.at[1, i], near_recv.at[side, i], (ctx, target))

    def project(i, carry):
        w_copy(i).wait()
        part[:, pl.ds(column(i), COLS)] = jnp.dot(att[...], w[i], preferred_element_type=F32).astype(BF16)
        far_copy(i).start()
        return carry

    lax.fori_loop(0, PIECES, project, 0)

    def send_near(i, carry):
        near_copy(i).start()
        return carry

    lax.fori_loop(0, PIECES, send_near, 0)

    def combine(i, carry):
        target = jnp.where(lax.rem(i, 2) == 0, right, left)
        far_copy(i).wait_recv()
        mine = part[rows(target), pl.ds(column(i), COLS)].astype(F32)
        comb[i] = (mine + far[i].astype(F32)).astype(BF16)
        comb_copy(i).start()
        return carry

    lax.fori_loop(0, PIECES, combine, 0)

    def add_up(i, carry):
        near_copy(i).wait_recv()
        comb_copy(i).wait_recv()
        mine = part[rows(me_y), pl.ds(column(i), COLS)].astype(F32)
        proj[:, pl.ds(column(i), COLS)] = (mine + near[0, i].astype(F32) + near[1, i].astype(F32)).astype(BF16)
        return carry

    lax.fori_loop(0, PIECES, add_up, 0)

    for role in range(NX):
        @pl.when(x == role)
        def _():
            for sems, *index in started[role]:
                remote(kv.at[ROW, 0], kv.at[ROW, 0], sems.at[*index], kv_recv.at[0, 0], sibling).wait_send()

    for j in range(2 * KV):
        sib_copy(kv.at[i8, j], x, j).wait_send()

    def drain(i, carry):
        far_copy(i).wait_send()
        near_copy(i).wait_send()
        comb_copy(i).wait_send()
        return carry

    lax.fori_loop(0, PIECES, drain, 0)


def hand_over(*refs):
    sources, targets, sems = refs[:3], refs[3:6], refs[6]
    copies = [pltpu.make_async_copy(a, b, sems.at[i]) for i, (a, b) in enumerate(zip(sources, targets))]
    for copy in copies:
        copy.start()
    for copy in copies:
        copy.wait()


def local(queries, keys, values, lengths, out_weight):
    hbm = pl.BlockSpec(memory_space=pl.ANY)
    dma = pltpu.SemaphoreType.DMA
    results = pl.pallas_call(
        kernel,
        out_shape=(
            pltpu.VMEM((T, HQ * HD), BF16),
            pltpu.VMEM((HQ, T), F32),
            pltpu.VMEM((OWNED, D), BF16),
        ),
        in_specs=[pl.BlockSpec(memory_space=pltpu.SMEM)] + [hbm] * 4,
        out_specs=(pl.BlockSpec(memory_space=pltpu.VMEM),) * 3,
        scratch_shapes=[
            pltpu.VMEM((T, HQ * HD), BF16),
            pltpu.VMEM((ROW + 1, 2 * KV, T, HD), BF16),
            pltpu.VMEM((2, KV, T, HD), BF16),
            pltpu.VMEM((PIECES, HQ * HD, COLS), BF16),
            pltpu.VMEM((T, HD), BF16),
            pltpu.VMEM((ROW + 1, T, HD), BF16),
            pltpu.VMEM((ROW + 1, HQ, T, T), F32),
            pltpu.VMEM((HQ, T, HD), F32),
            pltpu.VMEM((HQ, T, 2 * HD), F32),
            pltpu.VMEM((T, D), BF16),
            pltpu.VMEM((PIECES, OWNED, COLS), BF16),
            pltpu.VMEM((2, PIECES, OWNED, COLS), BF16),
            pltpu.VMEM((PIECES, OWNED, COLS), BF16),
            dma, dma((2 * KV,)), dma((PIECES,)),
            dma((2, 2 * KV)), dma((2, 3, 2 * KV)), dma((NX, 2 * KV)), dma((ROW, 2 * KV)), dma((2, KV)),
            dma((PIECES,)), dma((PIECES,)), dma((2, PIECES)), dma((2, PIECES)),
        ],
        compiler_params=pltpu.CompilerParams(
            collective_id=0, has_side_effects=True, vmem_limit_bytes=56 * 2**20
        ),
    )(lengths, queries, keys, values, out_weight)
    results = [pltpu.with_memory_space_constraint(r, pltpu.VMEM) for r in results]
    return pl.pallas_call(
        hand_over,
        out_shape=tuple(jax.ShapeDtypeStruct(r.shape, r.dtype) for r in results),
        in_specs=[pl.BlockSpec(memory_space=pltpu.VMEM)] * 3,
        out_specs=(hbm,) * 3,
        scratch_shapes=[dma((3,))],
    )(*results)


def solution(mesh):
    placed = (P("ctx", "head"), P("ctx", "head"), P("ctx", "head"), P(), P("head", None))
    return jax.shard_map(
        local,
        mesh=mesh,
        in_specs=placed,
        out_specs=(P("ctx", "head"), P("head", "ctx"), P(("ctx", "head"), None)),
        check_vma=False,
    )
```

```python
import functools

import jax
import jax.numpy as jnp
from jax import lax
from jax.experimental import pallas as pl
from jax.experimental.pallas import tpu as pltpu
from jax.sharding import PartitionSpec as P

HD = 128
T = 256
NX, NC, NY = 4, 2, 4
ROW = NX * NC
KV, GROUP = 2, 4
HQ = KV * GROUP
DOCS = 16
D = 4096
OWNED = T // NY
COLS = 512
PIECES = D // COLS
HALF = PIECES // 2
FAR = -1e30
MESH = pl.DeviceIdType.MESH
F32, BF16 = jnp.float32, jnp.bfloat16
SCALE = HD**-0.5
LOG2E = 1.4426950408889634


def kernel(
    len_ref, q_hbm, k_hbm, v_hbm, w_hbm,
    att, lse, proj,
    q, kv, w, qaug, kaug, score, top, acc, part, far, near, comb,
    q_sem, own_sem, w_sem,
    z_send, x_send, sib_send, kv_recv, far_send, far_recv, near_send, near_recv,
):
    ctx, me_y = lax.axis_index("ctx"), lax.axis_index("head")
    depth = lax.axis_size("ctx") // ROW
    z, i8 = ctx // ROW, lax.rem(ctx, ROW)
    x, c = i8 // NC, lax.rem(i8, NC)

    def head_columns(h):
        return pl.ds(h * HD if isinstance(h, int) else pl.multiple_of(h * HD, HD), HD)

    def at_x(d):
        return lax.rem(x + d, NX)

    def dev(zz, xx, cc):
        return (zz * ROW + xx * NC + cc, me_y)

    z_up, z_down = lax.rem(z + 1, depth), lax.rem(z + depth - 1, depth)
    right, left, across = (lax.rem(me_y + d, NY) for d in (1, NY - 1, 2))
    sibling = dev(z, x, 1 - c)

    has_prev, has_next = z > 0, z < depth - 1
    x_up, x_down, x_across = (dev(z, at_x(d), c) for d in (1, NX - 1, 2))

    barrier = pltpu.get_barrier_semaphore()

    def greet(peer):
        pl.semaphore_signal(barrier, inc=1, device_id=peer, device_id_type=MESH)

    for peer in (x_up, x_down, x_across, sibling, (ctx, right), (ctx, left)):
        greet(peer)
    others = [(has_prev, dev(z_down, x, c)), (has_next, dev(z_up, x, c))]
    others += [((x < 2) & has_prev, dev(z_down, at_x(2), c)), ((x >= 2) & has_next, dev(z_up, at_x(2), c))]
    for is_there, peer in others:
        pl.when(is_there)(functools.partial(greet, peer))

    own_src = [k_hbm.at[:, pl.ds(g * HD, HD)] for g in range(KV)]
    own_src += [v_hbm.at[:, pl.ds(g * HD, HD)] for g in range(KV)]
    q_copy = pltpu.make_async_copy(q_hbm, q, q_sem)
    own_copies = [pltpu.make_async_copy(own_src[j], kv.at[ROW, j], own_sem.at[j]) for j in range(2 * KV)]

    def column(i):
        return pl.multiple_of(lax.rem(i, 2) * (D // 2) + (i // 2) * COLS, COLS)

    def w_copy(i):
        return pltpu.make_async_copy(w_hbm.at[:, pl.ds(column(i), COLS)], w.at[i], w_sem.at[i])

    q_copy.start()
    for copy in own_copies:
        copy.start()

    pl.semaphore_wait(barrier, 6 + sum(is_there.astype(jnp.int32) for is_there, _ in others))

    def remote(src, dst, send, recv, device):
        return pltpu.make_async_remote_copy(
            src_ref=src, dst_ref=dst, send_sem=send, recv_sem=recv, device_id=device, device_id_type=MESH
        )

    slots = [origin * NC + c for origin in range(NX)]

    def sib_copy(src, origin, j):
        slot = origin * NC + c
        return remote(src, kv.at[slot, j], sib_send.at[origin, j], kv_recv.at[slot, j], sibling)

    def arrived(slot, j):
        remote(kv.at[slot, j], kv.at[slot, j], z_send.at[0, j], kv_recv.at[slot, j], sibling).wait_recv()

    started = [[] for _ in range(NX)]
    OWN, PREV, RELAY, FAR_X = range(4)
    UP, DOWN = range(2)

    def guarded(condition, act):
        if condition is None:
            act()
        else:
            pl.when(condition)(act)

    def send(role, condition, copy, *sem):
        copy.start()
        started[role].append((condition, sem))

    def along_x(role, condition, way, kind, src, dst, recv, j):
        target = x_across if kind == FAR_X else x_up if way == UP else x_down
        send(role, condition, remote(src, dst, x_send.at[way, kind, j], recv, target), x_send, way, kind, j)

    def block_along_x(role, condition, way, kind, origin, src, j):
        slot = slots[origin]
        along_x(role, condition, way, kind, src, kv.at[slot, j], kv_recv.at[slot, j], j)

    def up_z(role, kind, j):
        slot = slots[role]
        target = dev(z_up, at_x(2) if kind else x, c)
        copy = remote(own_src[j], kv.at[slot, j], z_send.at[kind, j], kv_recv.at[slot, j], target)
        send(role, has_next, copy, z_send, kind, j)

    def got(role, origin, j, *ways):
        condition = has_prev if origin > role else None

        def act():
            src = kv.at[slots[origin], j]
            arrived(slots[origin], j)
            for way in ways:
                block_along_x(role, condition, way, RELAY, origin, src, j)
            send(role, condition, sib_copy(src, origin, j), sib_send, origin, j)

        guarded(condition, act)

    def got_prev(role, j, *ways):
        def act():
            src = kv.at[slots[role], j]
            arrived(slots[role], j)
            for way in ways:
                block_along_x(role, has_prev, way, PREV, role, src, j)

            @pl.when(c == 1)
            def _():
                sib_copy(src, role, j).start()

        guarded(has_prev, act)

    def own_sends(role, b):
        for kind in (0, 1) if role >= 2 else (0,):
            for j in (b, b + 1):
                guarded(has_next, functools.partial(up_z, role, kind, j))
        for j in (b, b + 1):
            src = own_src[j]
            if role < 3:
                block_along_x(role, None, UP, OWN, role, src, j)
            if role == 0:
                block_along_x(role, None, DOWN, OWN, role, src, j)

            @pl.when(c == 0)
            def _():
                sib_copy(src, role, j).start()
        if role < 2:
            for j in (b, b + 1):
                block_along_x(role, None, UP, FAR_X, role, own_src[j], j)

    def prev(role, j):
        got_prev(role, j, *[[], [DOWN], [DOWN], [UP, DOWN]][role])

    def others_x(role, j):
        for d in (1, 3, 2):
            got(role, (role + d) % NX, j)

    def in_role(stage, b):
        for role in range(NX):
            pl.when(x == role)(functools.partial(stage, role, b))

    in_role(own_sends, 0)

    def there(slot):
        return has_prev | (slot < i8)

    def from_sibling(d, j):
        slot = at_x(d) * NC + 1 - c
        pl.when(there(slot))(lambda: arrived(slot, j))

    for slot in range(ROW):
        @pl.when(jnp.logical_not(there(slot)))
        def _():
            kv[slot] = jnp.zeros((2 * KV, T, HD), BF16)

    def w_start(i, carry):
        w_copy(i).start()
        return carry

    lax.fori_loop(0, PIECES, w_start, 0)

    lane = lax.broadcasted_iota(jnp.int32, (1, HD), 1)
    first = jnp.zeros((1, HD), jnp.int32)
    last = jnp.zeros((1, HD), jnp.int32)
    end = jnp.int32(0)
    for d in range(DOCS):
        first = jnp.where(lane == d, end, first)
        end = end + len_ref[d]
        last = jnp.where(lane == d, end, last)
    token = lax.broadcasted_iota(jnp.int32, (T, HD), 0)

    def inside(block):
        position = block * T + token
        return (position >= first) & (position < last)

    qaug[...] = jnp.where(inside(ctx), 1.0, 0.0).astype(BF16)

    same_slots = [at_x(d) * NC + c for d in (1, 2, 3)]
    other_slots = [at_x(d) * NC + 1 - c for d in (1, 2, 3)]
    block_slots = [ROW + 0 * x, i8, x * NC + 1 - c] + same_slots + other_slots

    def slot_of(n):
        return block_slots[n]

    for n in range(ROW + 1):
        slot = slot_of(n)
        block = jnp.where(slot < i8, z * ROW + slot, (z - 1) * ROW + slot)
        kaug[n] = jnp.where(inside(ctx if n == 0 else block), 0.0, FAR).astype(BF16)

    def scores(first_n, last_n, g):
        for n in range(first_n, last_n):
            keys = jnp.concatenate([kv[slot_of(n), g], kaug[n]], axis=1)
            for r in range(GROUP):
                h = g * GROUP + r
                queries = jnp.concatenate([q[:, head_columns(h)], qaug[...]], axis=1)
                s = lax.dot_general(queries, keys, (((1,), (1,)), ((), ())), preferred_element_type=F32)
                if n == 0:
                    row = lax.broadcasted_iota(jnp.int32, (T, T), 0)
                    col = lax.broadcasted_iota(jnp.int32, (T, T), 1)
                    s = jnp.where(col <= row, s, FAR)
                score[n, h] = s
                high = jnp.maximum(s[:, :HD], s[:, HD:])
                top[h] = high if n == 0 else jnp.maximum(top[h], high)

    def mix(first_n, g):
        values = [kv[slot_of(first_n + i), KV + g] for i in range(3)]
        values = jnp.concatenate([jnp.concatenate(values, axis=0), jnp.ones((3 * T, HD), BF16)], axis=1)
        for r in range(GROUP):
            h = g * GROUP + r
            high = jnp.concatenate([top[h], top[h]], axis=1)
            weight = [jnp.exp2((score[first_n + i, h] - high) * (SCALE * LOG2E)).astype(BF16) for i in range(3)]
            mixed = jnp.dot(jnp.concatenate(weight, axis=1), values, preferred_element_type=F32)
            acc[h] = mixed if first_n == 0 else acc[h] + mixed

    q_copy.wait()
    for copy in own_copies:
        copy.wait()

    def own_scores(g, carry):
        scores(0, 1, g)
        return carry

    def close_scores(g, carry):
        from_sibling(0, g)
        scores(1, 3, g)
        return carry

    def same_scores(g, carry):
        scores(3, 6, g)
        return carry

    def other_scores(g, carry):
        for d in (1, 3, 2):
            from_sibling(d, g)
        scores(6, 9, g)
        return carry

    def each_kv(step):
        lax.fori_loop(0, KV, step, 0)

    def close_mix(g):
        from_sibling(0, KV + g)
        mix(0, g)

    def other_mix(g):
        for d in (1, 3, 2):
            from_sibling(d, KV + g)
        mix(6, g)

    in_role(prev, 0)
    in_role(own_sends, KV)
    each_kv(own_scores)
    in_role(prev, 1)
    each_kv(close_scores)
    in_role(others_x, 0)
    in_role(prev, 2)
    in_role(others_x, 1)
    in_role(prev, 3)
    each_kv(same_scores)
    each_kv(other_scores)
    for h in range(HQ):
        top[h] = jnp.broadcast_to(jnp.max(top[h], axis=1, keepdims=True), (T, HD))
    close_mix(0)
    in_role(others_x, 2)
    mix(3, 0)
    close_mix(1)
    in_role(others_x, 3)
    mix(3, 1)
    other_mix(0)
    other_mix(1)

    sums = jnp.zeros((T, HD), F32)
    for h in range(HQ):
        total = acc[h, :, HD:]
        att[:, h * HD : (h + 1) * HD] = (acc[h, :, :HD] / total).astype(BF16)
        sums = jnp.where(lane == h, top[h] * SCALE + jnp.log(total), sums)
    lse[...] = sums.T[:HQ]

    def rows(y):
        return pl.ds(pl.multiple_of(y * OWNED, OWNED), OWNED)

    def far_copy(i):
        side = lax.rem(i, 2)
        target = jnp.where(side == 0, right, left)
        return remote(part.at[rows(across), pl.ds(column(i), COLS)], far.at[i], far_send.at[i], far_recv.at[i], (ctx, target))

    def near_copy(i):
        side = lax.rem(i, 2)
        target = jnp.where(side == 0, left, right)
        return remote(
            part.at[rows(target), pl.ds(column(i), COLS)], near.at[1 - side, i],
            near_send.at[0, i], near_recv.at[1 - side, i], (ctx, target),
        )

    def comb_copy(i):
        side = lax.rem(i, 2)
        target = jnp.where(side == 0, right, left)
        return remote(comb.at[i], near.at[side, i], near_send.at[1, i], near_recv.at[side, i], (ctx, target))

    def project(i, carry):
        w_copy(i).wait()
        part[:, pl.ds(column(i), COLS)] = jnp.dot(att[...], w[i], preferred_element_type=F32).astype(BF16)
        far_copy(i).start()
        return carry

    lax.fori_loop(0, PIECES, project, 0)

    def send_near(i, carry):
        near_copy(i).start()
        return carry

    def combine(i, carry):
        target = jnp.where(lax.rem(i, 2) == 0, right, left)
        far_copy(i).wait_recv()
        mine = part[rows(target), pl.ds(column(i), COLS)].astype(F32)
        comb[i] = (mine + far[i].astype(F32)).astype(BF16)
        comb_copy(i).start()
        return carry

    lax.fori_loop(0, PIECES, combine, 0)
    lax.fori_loop(0, PIECES, send_near, 0)

    def add_up(i, carry):
        near_copy(i).wait_recv()
        comb_copy(i).wait_recv()
        mine = part[rows(me_y), pl.ds(column(i), COLS)].astype(F32)
        proj[:, pl.ds(column(i), COLS)] = (mine + near[0, i].astype(F32) + near[1, i].astype(F32)).astype(BF16)
        return carry

    lax.fori_loop(0, PIECES, add_up, 0)

    def sent(sems, *index):
        remote(kv.at[ROW, 0], kv.at[ROW, 0], sems.at[*index], kv_recv.at[0, 0], sibling).wait_send()

    def settle(role, _):
        for condition in (None, has_prev, has_next):
            todo = [sem for when, sem in started[role] if when is condition]

            def act():
                for sem in todo:
                    sent(*sem)

            if todo:
                guarded(condition, act)

    in_role(settle, 0)

    @pl.when((c == 0) | has_prev)
    def _():
        for j in range(2 * KV):
            sent(sib_send, x, j)

    def drain(i, carry):
        far_copy(i).wait_send()
        near_copy(i).wait_send()
        comb_copy(i).wait_send()
        return carry

    lax.fori_loop(0, PIECES, drain, 0)


def hand_over(*refs):
    sources, targets, sems = refs[:3], refs[3:6], refs[6]
    copies = [pltpu.make_async_copy(a, b, sems.at[i]) for i, (a, b) in enumerate(zip(sources, targets))]
    for copy in copies:
        copy.start()
    for copy in copies:
        copy.wait()


def local(queries, keys, values, lengths, out_weight):
    hbm = pl.BlockSpec(memory_space=pl.ANY)
    dma = pltpu.SemaphoreType.DMA
    results = pl.pallas_call(
        kernel,
        out_shape=(
            pltpu.VMEM((T, HQ * HD), BF16),
            pltpu.VMEM((HQ, T), F32),
            pltpu.VMEM((OWNED, D), BF16),
        ),
        in_specs=[pl.BlockSpec(memory_space=pltpu.SMEM)] + [hbm] * 4,
        out_specs=(pl.BlockSpec(memory_space=pltpu.VMEM),) * 3,
        scratch_shapes=[
            pltpu.VMEM((T, HQ * HD), BF16),
            pltpu.VMEM((ROW + 1, 2 * KV, T, HD), BF16),
            pltpu.VMEM((PIECES, HQ * HD, COLS), BF16),
            pltpu.VMEM((T, HD), BF16),
            pltpu.VMEM((ROW + 1, T, HD), BF16),
            pltpu.VMEM((ROW + 1, HQ, T, T), F32),
            pltpu.VMEM((HQ, T, HD), F32),
            pltpu.VMEM((HQ, T, 2 * HD), F32),
            pltpu.VMEM((T, D), BF16),
            pltpu.VMEM((PIECES, OWNED, COLS), BF16),
            pltpu.VMEM((2, PIECES, OWNED, COLS), BF16),
            pltpu.VMEM((PIECES, OWNED, COLS), BF16),
            dma, dma((2 * KV,)), dma((PIECES,)),
            dma((2, 2 * KV)), dma((2, 4, 2 * KV)), dma((NX, 2 * KV)), dma((ROW, 2 * KV)),
            dma((PIECES,)), dma((PIECES,)), dma((2, PIECES)), dma((2, PIECES)),
        ],
        compiler_params=pltpu.CompilerParams(
            collective_id=0, has_side_effects=True, vmem_limit_bytes=56 * 2**20
        ),
    )(lengths, queries, keys, values, out_weight)
    results = [pltpu.with_memory_space_constraint(r, pltpu.VMEM) for r in results]
    return pl.pallas_call(
        hand_over,
        out_shape=tuple(jax.ShapeDtypeStruct(r.shape, r.dtype) for r in results),
        in_specs=[pl.BlockSpec(memory_space=pltpu.VMEM)] * 3,
        out_specs=(hbm,) * 3,
        scratch_shapes=[dma((3,))],
    )(*results)


def solution(mesh):
    placed = (P("ctx", "head"), P("ctx", "head"), P("ctx", "head"), P(), P("head", None))
    return jax.shard_map(
        local,
        mesh=mesh,
        in_specs=placed,
        out_specs=(P("ctx", "head"), P("head", "ctx"), P(("ctx", "head"), None)),
        check_vma=False,
    )
```

```python
import functools

import jax
import jax.numpy as jnp
from jax import lax
from jax.experimental import pallas as pl
from jax.experimental.pallas import tpu as pltpu
from jax.sharding import PartitionSpec as P

HD = 128
T = 256
NX, NC, NY = 4, 2, 4
ROW = NX * NC
KV, GROUP = 2, 4
HQ = KV * GROUP
DOCS = 16
D = 4096
OWNED = T // NY
COLS = 512
PIECES = D // COLS
HALF = PIECES // 2
FAR = -1e30
MESH = pl.DeviceIdType.MESH
F32, BF16 = jnp.float32, jnp.bfloat16
SCALE = HD**-0.5
LOG2E = 1.4426950408889634


def kernel(
    len_ref, q_hbm, k_hbm, v_hbm, w_hbm,
    att, lse, proj,
    q, kv, w, qaug, kaug, score, top, acc, part, far, near, comb,
    q_sem, own_sem, w_sem,
    z_send, x_send, sib_send, kv_recv, far_send, far_recv, near_send, near_recv,
):
    ctx, me_y = lax.axis_index("ctx"), lax.axis_index("head")
    depth = lax.axis_size("ctx") // ROW
    z, i8 = ctx // ROW, lax.rem(ctx, ROW)
    x, c = i8 // NC, lax.rem(i8, NC)

    def head_columns(h):
        return pl.ds(h * HD if isinstance(h, int) else pl.multiple_of(h * HD, HD), HD)

    def at_x(d):
        return lax.rem(x + d, NX)

    def dev(zz, xx, cc):
        return (zz * ROW + xx * NC + cc, me_y)

    z_up, z_down = lax.rem(z + 1, depth), lax.rem(z + depth - 1, depth)
    right, left, across = (lax.rem(me_y + d, NY) for d in (1, NY - 1, 2))
    sibling = dev(z, x, 1 - c)

    has_prev, has_next = z > 0, z < depth - 1
    x_up, x_down, x_across = (dev(z, at_x(d), c) for d in (1, NX - 1, 2))

    barrier = pltpu.get_barrier_semaphore()

    def greet(peer):
        pl.semaphore_signal(barrier, inc=1, device_id=peer, device_id_type=MESH)

    for peer in (x_up, x_down, x_across, sibling, (ctx, right), (ctx, left)):
        greet(peer)
    others = [(has_prev, dev(z_down, x, c)), (has_next, dev(z_up, x, c))]
    others += [((x < 2) & has_prev, dev(z_down, at_x(2), c)), ((x >= 2) & has_next, dev(z_up, at_x(2), c))]
    for is_there, peer in others:
        pl.when(is_there)(functools.partial(greet, peer))

    own_src = [k_hbm.at[:, pl.ds(g * HD, HD)] for g in range(KV)]
    own_src += [v_hbm.at[:, pl.ds(g * HD, HD)] for g in range(KV)]
    q_copy = pltpu.make_async_copy(q_hbm, q, q_sem)
    own_copies = [pltpu.make_async_copy(own_src[j], kv.at[ROW, j], own_sem.at[j]) for j in range(2 * KV)]

    def column(i):
        return pl.multiple_of(lax.rem(i, 2) * (D // 2) + (i // 2) * COLS, COLS)

    def w_copy(i):
        return pltpu.make_async_copy(w_hbm.at[:, pl.ds(column(i), COLS)], w.at[i], w_sem.at[i])

    q_copy.start()
    for copy in own_copies:
        copy.start()

    pl.semaphore_wait(barrier, 6 + sum(is_there.astype(jnp.int32) for is_there, _ in others))

    def remote(src, dst, send, recv, device):
        return pltpu.make_async_remote_copy(
            src_ref=src, dst_ref=dst, send_sem=send, recv_sem=recv, device_id=device, device_id_type=MESH
        )

    slots = [origin * NC + c for origin in range(NX)]

    def sib_copy(src, origin, j):
        slot = origin * NC + c
        return remote(src, kv.at[slot, j], sib_send.at[origin, j], kv_recv.at[slot, j], sibling)

    def arrived(slot, j):
        remote(kv.at[slot, j], kv.at[slot, j], z_send.at[0, j], kv_recv.at[slot, j], sibling).wait_recv()

    started = [[] for _ in range(NX)]
    OWN, PREV, RELAY, FAR_X = range(4)
    UP, DOWN = range(2)

    def guarded(condition, act):
        if condition is None:
            act()
        else:
            pl.when(condition)(act)

    def send(role, condition, copy, *sem):
        copy.start()
        started[role].append((condition, sem))

    def along_x(role, condition, way, kind, src, dst, recv, j):
        target = x_across if kind == FAR_X else x_up if way == UP else x_down
        send(role, condition, remote(src, dst, x_send.at[way, kind, j], recv, target), x_send, way, kind, j)

    def block_along_x(role, condition, way, kind, origin, src, j):
        slot = slots[origin]
        along_x(role, condition, way, kind, src, kv.at[slot, j], kv_recv.at[slot, j], j)

    def up_z(role, kind, j):
        slot = slots[role]
        target = dev(z_up, at_x(2) if kind else x, c)
        copy = remote(own_src[j], kv.at[slot, j], z_send.at[kind, j], kv_recv.at[slot, j], target)
        send(role, has_next, copy, z_send, kind, j)

    def got(role, origin, j, *ways):
        condition = has_prev if origin > role else None

        def act():
            src = kv.at[slots[origin], j]
            arrived(slots[origin], j)
            for way in ways:
                block_along_x(role, condition, way, RELAY, origin, src, j)
            send(role, condition, sib_copy(src, origin, j), sib_send, origin, j)

        guarded(condition, act)

    def got_prev(role, j, *ways):
        def act():
            src = kv.at[slots[role], j]
            arrived(slots[role], j)
            for way in ways:
                block_along_x(role, has_prev, way, PREV, role, src, j)

            @pl.when(c == 1)
            def _():
                sib_copy(src, role, j).start()

        guarded(has_prev, act)

    def own_sends(role, _):
        for pair in ((0, 1), (2, 3)):
            for kind in (0, 1) if role >= 2 else (0,):
                for j in pair:
                    guarded(has_next, functools.partial(up_z, role, kind, j))
        for pair in ((0, 1), (2, 3)):
            for j in pair:
                src = own_src[j]
                if role < 3:
                    block_along_x(role, None, UP, OWN, role, src, j)
                if role == 0:
                    block_along_x(role, None, DOWN, OWN, role, src, j)

                @pl.when(c == 0)
                def _():
                    sib_copy(src, role, j).start()
            if role < 2:
                for j in pair:
                    block_along_x(role, None, UP, FAR_X, role, own_src[j], j)

    def prev(role, j):
        got_prev(role, j, *[[], [DOWN], [DOWN], [UP, DOWN]][role])

    def others_x(role, j):
        for d in (1, 3, 2):
            got(role, (role + d) % NX, j)

    def in_role(stage, b):
        for role in range(NX):
            pl.when(x == role)(functools.partial(stage, role, b))

    in_role(own_sends, 0)

    def there(slot):
        return has_prev | (slot < i8)

    def from_sibling(d, j):
        slot = at_x(d) * NC + 1 - c
        pl.when(there(slot))(lambda: arrived(slot, j))

    for slot in range(ROW):
        @pl.when(jnp.logical_not(there(slot)))
        def _():
            kv[slot] = jnp.zeros((2 * KV, T, HD), BF16)

    def w_start(i, carry):
        w_copy(i).start()
        return carry

    lax.fori_loop(0, PIECES, w_start, 0)

    lane = lax.broadcasted_iota(jnp.int32, (1, HD), 1)
    first = jnp.zeros((1, HD), jnp.int32)
    last = jnp.zeros((1, HD), jnp.int32)
    end = jnp.int32(0)
    for d in range(DOCS):
        first = jnp.where(lane == d, end, first)
        end = end + len_ref[d]
        last = jnp.where(lane == d, end, last)
    token = lax.broadcasted_iota(jnp.int32, (T, HD), 0)

    def inside(block):
        position = block * T + token
        return (position >= first) & (position < last)

    qaug[...] = jnp.where(inside(ctx), 1.0, 0.0).astype(BF16)

    same_slots = [at_x(d) * NC + c for d in (1, 2, 3)]
    other_slots = [at_x(d) * NC + 1 - c for d in (1, 2, 3)]
    block_slots = [ROW + 0 * x, i8, x * NC + 1 - c] + same_slots + other_slots

    def slot_of(n):
        return block_slots[n]

    for n in range(ROW + 1):
        slot = slot_of(n)
        block = jnp.where(slot < i8, z * ROW + slot, (z - 1) * ROW + slot)
        kaug[n] = jnp.where(inside(ctx if n == 0 else block), 0.0, FAR).astype(BF16)

    def scores(first_n, last_n, g):
        for n in range(first_n, last_n):
            keys = jnp.concatenate([kv[slot_of(n), g], kaug[n]], axis=1)
            for r in range(GROUP):
                h = g * GROUP + r
                queries = jnp.concatenate([q[:, head_columns(h)], qaug[...]], axis=1)
                s = lax.dot_general(queries, keys, (((1,), (1,)), ((), ())), preferred_element_type=F32)
                if n == 0:
                    row = lax.broadcasted_iota(jnp.int32, (T, T), 0)
                    col = lax.broadcasted_iota(jnp.int32, (T, T), 1)
                    s = jnp.where(col <= row, s, FAR)
                score[n, h] = s
                high = jnp.maximum(s[:, :HD], s[:, HD:])
                top[h] = high if n == 0 else jnp.maximum(top[h], high)

    def mix(first_n, g):
        values = [kv[slot_of(first_n + i), KV + g] for i in range(3)]
        values = jnp.concatenate([jnp.concatenate(values, axis=0), jnp.ones((3 * T, HD), BF16)], axis=1)
        for r in range(GROUP):
            h = g * GROUP + r
            high = jnp.concatenate([top[h], top[h]], axis=1)
            weight = [jnp.exp2((score[first_n + i, h] - high) * (SCALE * LOG2E)).astype(BF16) for i in range(3)]
            mixed = jnp.dot(jnp.concatenate(weight, axis=1), values, preferred_element_type=F32)
            acc[h] = mixed if first_n == 0 else acc[h] + mixed

    q_copy.wait()
    for copy in own_copies:
        copy.wait()

    def own_scores(g, carry):
        scores(0, 1, g)
        return carry

    def close_scores(g, carry):
        from_sibling(0, g)
        scores(1, 3, g)
        return carry

    def same_scores(g, carry):
        scores(3, 6, g)
        return carry

    def other_scores(g, carry):
        for d in (1, 3, 2):
            from_sibling(d, g)
        scores(6, 9, g)
        return carry

    def each_kv(step):
        lax.fori_loop(0, KV, step, 0)

    def close_mix(g):
        from_sibling(0, KV + g)
        mix(0, g)

    def other_mix(g):
        for d in (1, 3, 2):
            from_sibling(d, KV + g)
        mix(6, g)

    in_role(prev, 0)
    each_kv(own_scores)
    in_role(prev, 1)
    each_kv(close_scores)
    in_role(prev, 2)
    in_role(others_x, 0)
    in_role(prev, 3)
    in_role(others_x, 1)
    each_kv(same_scores)
    each_kv(other_scores)
    for h in range(HQ):
        top[h] = jnp.broadcast_to(jnp.max(top[h], axis=1, keepdims=True), (T, HD))
    close_mix(0)
    in_role(others_x, 2)
    mix(3, 0)
    close_mix(1)
    in_role(others_x, 3)
    mix(3, 1)
    def divide(g):
        for h in range(g * GROUP, (g + 1) * GROUP):
            att[:, head_columns(h)] = (acc[h, :, :HD] / acc[h, :, HD:]).astype(BF16)

    other_mix(0)
    divide(0)
    other_mix(1)
    divide(1)

    def rows(y):
        return pl.ds(pl.multiple_of(y * OWNED, OWNED), OWNED)

    def far_copy(i):
        side = lax.rem(i, 2)
        target = jnp.where(side == 0, right, left)
        return remote(part.at[rows(across), pl.ds(column(i), COLS)], far.at[i], far_send.at[i], far_recv.at[i], (ctx, target))

    def near_copy(i):
        side = lax.rem(i, 2)
        target = jnp.where(side == 0, left, right)
        return remote(
            part.at[rows(target), pl.ds(column(i), COLS)], near.at[1 - side, i],
            near_send.at[0, i], near_recv.at[1 - side, i], (ctx, target),
        )

    def comb_copy(i):
        side = lax.rem(i, 2)
        target = jnp.where(side == 0, right, left)
        return remote(comb.at[i], near.at[side, i], near_send.at[1, i], near_recv.at[side, i], (ctx, target))

    def project(i, carry):
        w_copy(i).wait()
        part[:, pl.ds(column(i), COLS)] = jnp.dot(att[...], w[i], preferred_element_type=F32).astype(BF16)
        far_copy(i).start()
        return carry

    lax.fori_loop(0, PIECES, project, 0)

    def send_near(i, carry):
        near_copy(i).start()
        return carry

    def combine(i, carry):
        target = jnp.where(lax.rem(i, 2) == 0, right, left)
        far_copy(i).wait_recv()
        mine = part[rows(target), pl.ds(column(i), COLS)].astype(F32)
        comb[i] = (mine + far[i].astype(F32)).astype(BF16)
        comb_copy(i).start()
        return carry

    lax.fori_loop(0, PIECES, combine, 0)
    lax.fori_loop(0, PIECES, send_near, 0)

    sums = jnp.zeros((T, HD), F32)
    for h in range(HQ):
        sums = jnp.where(lane == h, top[h] * SCALE + jnp.log(acc[h, :, HD:]), sums)
    lse[...] = sums.T[:HQ]

    def sent(sems, *index):
        remote(kv.at[ROW, 0], kv.at[ROW, 0], sems.at[*index], kv_recv.at[0, 0], sibling).wait_send()

    def settle(role, _):
        for condition in (None, has_prev, has_next):
            todo = [sem for when, sem in started[role] if when is condition]

            def act():
                for sem in todo:
                    sent(*sem)

            if todo:
                guarded(condition, act)

    in_role(settle, 0)

    @pl.when((c == 0) | has_prev)
    def _():
        for j in range(2 * KV):
            sent(sib_send, x, j)

    def far_sent(i, carry):
        far_copy(i).wait_send()
        return carry

    lax.fori_loop(0, PIECES, far_sent, 0)

    def add_up(i, carry):
        comb_copy(i).wait()
        near_copy(i).wait()
        mine = part[rows(me_y), pl.ds(column(i), COLS)].astype(F32)
        proj[:, pl.ds(column(i), COLS)] = (mine + near[0, i].astype(F32) + near[1, i].astype(F32)).astype(BF16)
        return carry

    lax.fori_loop(0, PIECES, add_up, 0)


def hand_over(*refs):
    sources, targets, sems = refs[:3], refs[3:6], refs[6]
    copies = [pltpu.make_async_copy(a, b, sems.at[i]) for i, (a, b) in enumerate(zip(sources, targets))]
    for copy in copies:
        copy.start()
    for copy in copies:
        copy.wait()


def local(queries, keys, values, lengths, out_weight):
    hbm = pl.BlockSpec(memory_space=pl.ANY)
    dma = pltpu.SemaphoreType.DMA
    results = pl.pallas_call(
        kernel,
        out_shape=(
            pltpu.VMEM((T, HQ * HD), BF16),
            pltpu.VMEM((HQ, T), F32),
            pltpu.VMEM((OWNED, D), BF16),
        ),
        in_specs=[pl.BlockSpec(memory_space=pltpu.SMEM)] + [hbm] * 4,
        out_specs=(pl.BlockSpec(memory_space=pltpu.VMEM),) * 3,
        scratch_shapes=[
            pltpu.VMEM((T, HQ * HD), BF16),
            pltpu.VMEM((ROW + 1, 2 * KV, T, HD), BF16),
            pltpu.VMEM((PIECES, HQ * HD, COLS), BF16),
            pltpu.VMEM((T, HD), BF16),
            pltpu.VMEM((ROW + 1, T, HD), BF16),
            pltpu.VMEM((ROW + 1, HQ, T, T), F32),
            pltpu.VMEM((HQ, T, HD), F32),
            pltpu.VMEM((HQ, T, 2 * HD), F32),
            pltpu.VMEM((T, D), BF16),
            pltpu.VMEM((PIECES, OWNED, COLS), BF16),
            pltpu.VMEM((2, PIECES, OWNED, COLS), BF16),
            pltpu.VMEM((PIECES, OWNED, COLS), BF16),
            dma, dma((2 * KV,)), dma((PIECES,)),
            dma((2, 2 * KV)), dma((2, 4, 2 * KV)), dma((NX, 2 * KV)), dma((ROW, 2 * KV)),
            dma((PIECES,)), dma((PIECES,)), dma((2, PIECES)), dma((2, PIECES)),
        ],
        compiler_params=pltpu.CompilerParams(
            collective_id=0, has_side_effects=True, vmem_limit_bytes=56 * 2**20
        ),
    )(lengths, queries, keys, values, out_weight)
    results = [pltpu.with_memory_space_constraint(r, pltpu.VMEM) for r in results]
    return pl.pallas_call(
        hand_over,
        out_shape=tuple(jax.ShapeDtypeStruct(r.shape, r.dtype) for r in results),
        in_specs=[pl.BlockSpec(memory_space=pltpu.VMEM)] * 3,
        out_specs=(hbm,) * 3,
        scratch_shapes=[dma((3,))],
    )(*results)


def solution(mesh):
    placed = (P("ctx", "head"), P("ctx", "head"), P("ctx", "head"), P(), P("head", None))
    return jax.shard_map(
        local,
        mesh=mesh,
        in_specs=placed,
        out_specs=(P("ctx", "head"), P("head", "ctx"), P(("ctx", "head"), None)),
        check_vma=False,
    )
```

```python
import functools

import jax
import jax.numpy as jnp
from jax import lax
from jax.experimental import pallas as pl
from jax.experimental.pallas import tpu as pltpu
from jax.sharding import PartitionSpec as P

HD = 128
T = 256
NX, NC, NY = 4, 2, 4
ROW = NX * NC
KV, GROUP = 2, 4
HQ = KV * GROUP
DOCS = 16
D = 4096
OWNED = T // NY
COLS = 512
PIECES = D // COLS
HALF = PIECES // 2
FAR = -1e30
MESH = pl.DeviceIdType.MESH
F32, BF16 = jnp.float32, jnp.bfloat16
SCALE = HD**-0.5
LOG2E = 1.4426950408889634


def kernel(
    len_ref, q_hbm, k_hbm, v_hbm, w_hbm,
    att, lse, proj,
    q, kv, w, qaug, kaug, score, top, acc, part, far, near, comb,
    q_sem, own_sem, w_sem,
    z_send, x_send, sib_send, kv_recv, far_send, far_recv, near_send, near_recv,
):
    ctx, me_y = lax.axis_index("ctx"), lax.axis_index("head")
    depth = lax.axis_size("ctx") // ROW
    z, i8 = ctx // ROW, lax.rem(ctx, ROW)
    x, c = i8 // NC, lax.rem(i8, NC)

    def head_columns(h):
        return pl.ds(h * HD if isinstance(h, int) else pl.multiple_of(h * HD, HD), HD)

    def at_x(d):
        return lax.rem(x + d, NX)

    def dev(zz, xx, cc):
        return (zz * ROW + xx * NC + cc, me_y)

    z_up, z_down = lax.rem(z + 1, depth), lax.rem(z + depth - 1, depth)
    right, left, across = (lax.rem(me_y + d, NY) for d in (1, NY - 1, 2))
    sibling = dev(z, x, 1 - c)

    has_prev, has_next = z > 0, z < depth - 1
    x_up, x_down, x_across = (dev(z, at_x(d), c) for d in (1, NX - 1, 2))

    barrier = pltpu.get_barrier_semaphore()

    def greet(peer):
        pl.semaphore_signal(barrier, inc=1, device_id=peer, device_id_type=MESH)

    for peer in (x_up, x_down, x_across, sibling, (ctx, right), (ctx, left)):
        greet(peer)
    others = [(has_prev, dev(z_down, x, c)), (has_next, dev(z_up, x, c))]
    others += [((x < 2) & has_prev, dev(z_down, at_x(2), c)), ((x >= 2) & has_next, dev(z_up, at_x(2), c))]
    for is_there, peer in others:
        pl.when(is_there)(functools.partial(greet, peer))

    own_src = [k_hbm.at[:, pl.ds(g * HD, HD)] for g in range(KV)]
    own_src += [v_hbm.at[:, pl.ds(g * HD, HD)] for g in range(KV)]
    q_copy = pltpu.make_async_copy(q_hbm, q, q_sem)
    own_copies = [pltpu.make_async_copy(own_src[j], kv.at[ROW, j], own_sem.at[j]) for j in range(2 * KV)]

    def column(i):
        return pl.multiple_of(lax.rem(i, 2) * (D // 2) + (i // 2) * COLS, COLS)

    def w_copy(i):
        return pltpu.make_async_copy(w_hbm.at[:, pl.ds(column(i), COLS)], w.at[i], w_sem.at[i])

    q_copy.start()
    for copy in own_copies:
        copy.start()

    pl.semaphore_wait(barrier, 6 + sum(is_there.astype(jnp.int32) for is_there, _ in others))

    def remote(src, dst, send, recv, device):
        return pltpu.make_async_remote_copy(
            src_ref=src, dst_ref=dst, send_sem=send, recv_sem=recv, device_id=device, device_id_type=MESH
        )

    slots = [origin * NC + c for origin in range(NX)]

    def sib_copy(src, origin, j):
        slot = origin * NC + c
        return remote(src, kv.at[slot, j], sib_send.at[origin, j], kv_recv.at[slot, j], sibling)

    def arrived(slot, j):
        remote(kv.at[slot, j], kv.at[slot, j], z_send.at[0, j], kv_recv.at[slot, j], sibling).wait_recv()

    started = [[] for _ in range(NX)]
    OWN, PREV, RELAY, FAR_X = range(4)
    UP, DOWN = range(2)

    def guarded(condition, act):
        if condition is None:
            act()
        else:
            pl.when(condition)(act)

    def send(role, condition, copy, *sem):
        copy.start()
        started[role].append((condition, sem))

    def along_x(role, condition, way, kind, src, dst, recv, j):
        target = x_across if kind == FAR_X else x_up if way == UP else x_down
        send(role, condition, remote(src, dst, x_send.at[way, kind, j], recv, target), x_send, way, kind, j)

    def block_along_x(role, condition, way, kind, origin, src, j):
        slot = slots[origin]
        along_x(role, condition, way, kind, src, kv.at[slot, j], kv_recv.at[slot, j], j)

    def up_z(role, kind, j):
        slot = slots[role]
        target = dev(z_up, at_x(2) if kind else x, c)
        copy = remote(own_src[j], kv.at[slot, j], z_send.at[kind, j], kv_recv.at[slot, j], target)
        send(role, has_next, copy, z_send, kind, j)

    def got(role, origin, j, *ways):
        condition = has_prev if origin > role else None

        def act():
            src = kv.at[slots[origin], j]
            arrived(slots[origin], j)
            for way in ways:
                block_along_x(role, condition, way, RELAY, origin, src, j)
            send(role, condition, sib_copy(src, origin, j), sib_send, origin, j)

        guarded(condition, act)

    def got_prev(role, j, *ways):
        def act():
            src = kv.at[slots[role], j]
            arrived(slots[role], j)
            for way in ways:
                block_along_x(role, has_prev, way, PREV, role, src, j)

            @pl.when(c == 1)
            def _():
                sib_copy(src, role, j).start()

        guarded(has_prev, act)

    def own_sends(role, _):
        for pair in ((0, 1), (2, 3)):
            for kind in (0, 1) if role >= 2 else (0,):
                for j in pair:
                    guarded(has_next, functools.partial(up_z, role, kind, j))
            for j in pair:
                src = own_src[j]
                if role < 3:
                    block_along_x(role, None, UP, OWN, role, src, j)
                if role == 0:
                    block_along_x(role, None, DOWN, OWN, role, src, j)

                @pl.when(c == 0)
                def _():
                    sib_copy(src, role, j).start()
            if role < 2:
                for j in pair:
                    block_along_x(role, None, UP, FAR_X, role, own_src[j], j)

    def prev(role, j):
        got_prev(role, j, *[[], [DOWN], [DOWN], [UP, DOWN]][role])

    def others_x(role, j):
        for d in (1, 3, 2):
            got(role, (role + d) % NX, j)

    def in_role(stage, b):
        for role in range(NX):
            pl.when(x == role)(functools.partial(stage, role, b))

    in_role(own_sends, 0)

    def there(slot):
        return has_prev | (slot < i8)

    def from_sibling(d, j):
        slot = at_x(d) * NC + 1 - c
        pl.when(there(slot))(lambda: arrived(slot, j))

    for slot in range(ROW):
        @pl.when(jnp.logical_not(there(slot)))
        def _():
            kv[slot] = jnp.zeros((2 * KV, T, HD), BF16)

    def w_start(i, carry):
        w_copy(i).start()
        return carry


    lane = lax.broadcasted_iota(jnp.int32, (1, HD), 1)
    first = jnp.zeros((1, HD), jnp.int32)
    last = jnp.zeros((1, HD), jnp.int32)
    end = jnp.int32(0)
    for d in range(DOCS):
        first = jnp.where(lane == d, end, first)
        end = end + len_ref[d]
        last = jnp.where(lane == d, end, last)
    token = lax.broadcasted_iota(jnp.int32, (T, HD), 0)

    def inside(block):
        position = block * T + token
        return (position >= first) & (position < last)

    qaug[...] = jnp.where(inside(ctx), 1.0, 0.0).astype(BF16)

    same_slots = [at_x(d) * NC + c for d in (1, 2, 3)]
    other_slots = [at_x(d) * NC + 1 - c for d in (1, 2, 3)]
    block_slots = [ROW + 0 * x, i8, x * NC + 1 - c] + same_slots + other_slots

    def slot_of(n):
        return block_slots[n]

    for n in range(ROW + 1):
        slot = slot_of(n)
        block = jnp.where(slot < i8, z * ROW + slot, (z - 1) * ROW + slot)
        kaug[n] = jnp.where(inside(ctx if n == 0 else block), 0.0, FAR).astype(BF16)

    def scores(first_n, last_n, g):
        for n in range(first_n, last_n):
            keys = jnp.concatenate([kv[slot_of(n), g], kaug[n]], axis=1)
            for r in range(GROUP):
                h = g * GROUP + r
                queries = jnp.concatenate([q[:, head_columns(h)], qaug[...]], axis=1)
                s = lax.dot_general(queries, keys, (((1,), (1,)), ((), ())), preferred_element_type=F32)
                if n == 0:
                    row = lax.broadcasted_iota(jnp.int32, (T, T), 0)
                    col = lax.broadcasted_iota(jnp.int32, (T, T), 1)
                    s = jnp.where(col <= row, s, FAR)
                score[n, h] = s
                high = jnp.maximum(s[:, :HD], s[:, HD:])
                top[h] = high if n == 0 else jnp.maximum(top[h], high)

    def mix(first_n, g):
        values = [kv[slot_of(first_n + i), KV + g] for i in range(3)]
        values = jnp.concatenate([jnp.concatenate(values, axis=0), jnp.ones((3 * T, HD), BF16)], axis=1)
        for r in range(GROUP):
            h = g * GROUP + r
            high = jnp.concatenate([top[h], top[h]], axis=1)
            weight = [jnp.exp2((score[first_n + i, h] - high) * (SCALE * LOG2E)).astype(BF16) for i in range(3)]
            mixed = jnp.dot(jnp.concatenate(weight, axis=1), values, preferred_element_type=F32)
            acc[h] = mixed if first_n == 0 else acc[h] + mixed

    q_copy.wait()
    for copy in own_copies:
        copy.wait()

    def own_scores(g, carry):
        scores(0, 1, g)
        return carry

    def close_scores(g, carry):
        from_sibling(0, g)
        scores(1, 3, g)
        return carry

    def same_scores(g, carry):
        scores(3, 6, g)
        return carry

    def other_scores(g, carry):
        for d in (1, 3, 2):
            from_sibling(d, g)
        scores(6, 9, g)
        return carry

    def each_kv(step):
        lax.fori_loop(0, KV, step, 0)

    def close_mix(g):
        from_sibling(0, KV + g)
        mix(0, g)

    def other_mix(g):
        for d in (1, 3, 2):
            from_sibling(d, KV + g)
        mix(6, g)

    in_role(prev, 0)
    each_kv(own_scores)
    in_role(prev, 1)
    each_kv(close_scores)
    in_role(prev, 2)
    in_role(others_x, 0)
    lax.fori_loop(0, PIECES, w_start, 0)
    in_role(prev, 3)
    in_role(others_x, 1)
    each_kv(same_scores)
    each_kv(other_scores)
    for h in range(HQ):
        top[h] = jnp.broadcast_to(jnp.max(top[h], axis=1, keepdims=True), (T, HD))
    close_mix(0)
    in_role(others_x, 2)
    mix(3, 0)
    close_mix(1)
    in_role(others_x, 3)
    mix(3, 1)
    def divide(g):
        for h in range(g * GROUP, (g + 1) * GROUP):
            att[:, head_columns(h)] = (acc[h, :, :HD] / acc[h, :, HD:]).astype(BF16)

    other_mix(0)
    divide(0)
    other_mix(1)
    divide(1)

    def rows(y):
        return pl.ds(pl.multiple_of(y * OWNED, OWNED), OWNED)

    def far_copy(i):
        side = lax.rem(i, 2)
        target = jnp.where(side == 0, right, left)
        return remote(part.at[rows(across), pl.ds(column(i), COLS)], far.at[i], far_send.at[i], far_recv.at[i], (ctx, target))

    def near_copy(i):
        side = lax.rem(i, 2)
        target = jnp.where(side == 0, left, right)
        return remote(
            part.at[rows(target), pl.ds(column(i), COLS)], near.at[1 - side, i],
            near_send.at[0, i], near_recv.at[1 - side, i], (ctx, target),
        )

    def comb_copy(i):
        side = lax.rem(i, 2)
        target = jnp.where(side == 0, right, left)
        return remote(comb.at[i], near.at[side, i], near_send.at[1, i], near_recv.at[side, i], (ctx, target))

    def project(i, carry):
        w_copy(i).wait()
        part[:, pl.ds(column(i), COLS)] = jnp.dot(att[...], w[i], preferred_element_type=F32).astype(BF16)
        far_copy(i).start()
        return carry

    lax.fori_loop(0, PIECES, project, 0)

    def send_near(i, carry):
        near_copy(i).start()
        return carry

    def combine(i, carry):
        target = jnp.where(lax.rem(i, 2) == 0, right, left)
        far_copy(i).wait_recv()
        mine = part[rows(target), pl.ds(column(i), COLS)].astype(F32)
        comb[i] = (mine + far[i].astype(F32)).astype(BF16)
        comb_copy(i).start()
        return carry

    lax.fori_loop(0, PIECES, combine, 0)
    lax.fori_loop(0, PIECES, send_near, 0)

    sums = jnp.zeros((T, HD), F32)
    for h in range(HQ):
        sums = jnp.where(lane == h, top[h] * SCALE + jnp.log(acc[h, :, HD:]), sums)
    lse[...] = sums.T[:HQ]

    def sent(sems, *index):
        remote(kv.at[ROW, 0], kv.at[ROW, 0], sems.at[*index], kv_recv.at[0, 0], sibling).wait_send()

    def settle(role, _):
        for condition in (None, has_prev, has_next):
            todo = [sem for when, sem in started[role] if when is condition]

            def act():
                for sem in todo:
                    sent(*sem)

            if todo:
                guarded(condition, act)

    in_role(settle, 0)

    @pl.when((c == 0) | has_prev)
    def _():
        for j in range(2 * KV):
            sent(sib_send, x, j)

    def far_sent(i, carry):
        far_copy(i).wait_send()
        return carry

    lax.fori_loop(0, PIECES, far_sent, 0)

    def add_up(i, carry):
        comb_copy(i).wait()
        near_copy(i).wait()
        mine = part[rows(me_y), pl.ds(column(i), COLS)].astype(F32)
        proj[:, pl.ds(column(i), COLS)] = (mine + near[0, i].astype(F32) + near[1, i].astype(F32)).astype(BF16)
        return carry

    lax.fori_loop(0, PIECES, add_up, 0)


def hand_over(*refs):
    sources, targets, sems = refs[:3], refs[3:6], refs[6]
    copies = [pltpu.make_async_copy(a, b, sems.at[i]) for i, (a, b) in enumerate(zip(sources, targets))]
    for copy in copies:
        copy.start()
    for copy in copies:
        copy.wait()


def local(queries, keys, values, lengths, out_weight):
    hbm = pl.BlockSpec(memory_space=pl.ANY)
    dma = pltpu.SemaphoreType.DMA
    results = pl.pallas_call(
        kernel,
        out_shape=(
            pltpu.VMEM((T, HQ * HD), BF16),
            pltpu.VMEM((HQ, T), F32),
            pltpu.VMEM((OWNED, D), BF16),
        ),
        in_specs=[pl.BlockSpec(memory_space=pltpu.SMEM)] + [hbm] * 4,
        out_specs=(pl.BlockSpec(memory_space=pltpu.VMEM),) * 3,
        scratch_shapes=[
            pltpu.VMEM((T, HQ * HD), BF16),
            pltpu.VMEM((ROW + 1, 2 * KV, T, HD), BF16),
            pltpu.VMEM((PIECES, HQ * HD, COLS), BF16),
            pltpu.VMEM((T, HD), BF16),
            pltpu.VMEM((ROW + 1, T, HD), BF16),
            pltpu.VMEM((ROW + 1, HQ, T, T), F32),
            pltpu.VMEM((HQ, T, HD), F32),
            pltpu.VMEM((HQ, T, 2 * HD), F32),
            pltpu.VMEM((T, D), BF16),
            pltpu.VMEM((PIECES, OWNED, COLS), BF16),
            pltpu.VMEM((2, PIECES, OWNED, COLS), BF16),
            pltpu.VMEM((PIECES, OWNED, COLS), BF16),
            dma, dma((2 * KV,)), dma((PIECES,)),
            dma((2, 2 * KV)), dma((2, 4, 2 * KV)), dma((NX, 2 * KV)), dma((ROW, 2 * KV)),
            dma((PIECES,)), dma((PIECES,)), dma((2, PIECES)), dma((2, PIECES)),
        ],
        compiler_params=pltpu.CompilerParams(
            collective_id=0, has_side_effects=True, vmem_limit_bytes=56 * 2**20
        ),
    )(lengths, queries, keys, values, out_weight)
    results = [pltpu.with_memory_space_constraint(r, pltpu.VMEM) for r in results]
    return pl.pallas_call(
        hand_over,
        out_shape=tuple(jax.ShapeDtypeStruct(r.shape, r.dtype) for r in results),
        in_specs=[pl.BlockSpec(memory_space=pltpu.VMEM)] * 3,
        out_specs=(hbm,) * 3,
        scratch_shapes=[dma((3,))],
    )(*results)


def solution(mesh):
    placed = (P("ctx", "head"), P("ctx", "head"), P("ctx", "head"), P(), P("head", None))
    return jax.shard_map(
        local,
        mesh=mesh,
        in_specs=placed,
        out_specs=(P("ctx", "head"), P("head", "ctx"), P(("ctx", "head"), None)),
        check_vma=False,
    )
```
